32 devices in a mesh: sample: 8 (over y, x, core), space: 4 (over z).
Axes of the slice: x: 2, y: 2, z: 4, core: 2. Of those that a mesh axis runs over, the one named last changes fastest.
Arguments:
- volumes: bfloat16 [8, 32, 16, 16, 128], P('sample', None, 'space'), may hold values from -360 to 360
- depth_kernel: float32 [32, 27], replicated, may hold values from -1.25 to 1.25
- point_weight: bfloat16 [32, 32], replicated, may hold values from -1 to 1
- cotangent: bfloat16 [8, 32, 16, 16, 128], P('sample', None, 'space'), may hold values from -4.1 to 4.1
Outputs:
- whitened: bfloat16 [8, 32, 16, 16, 128], P('sample', None, 'space')
- d_volumes: bfloat16 [8, 32, 16, 16, 128], P('sample', None, 'space')
- d_point: float32 [32, 32], replicated
- d_kernel: float32 [32, 27], replicated
The draws below stay inside these ranges and needn't reach their ends.
All inputs are finite; a program needn't handle non-finite values.
Results may differ from the reference program's by a relative error of at most 0.0067.
Values may be sent and summed in bfloat16 or wider, within the bound.
A program may use at most 64 MiB of HBM per device.

```python
import math
from functools import partial
import jax
import jax.numpy as jnp
from jax import lax

C = 32
GSIZE = 16
NEWTON = 5
HY = 16
WX = 128
GROUPS = 2
VOLUMES = 8
NZ = 16
COUNT = 262144


def draw_volumes(key, part):
    keys = jax.random.split(key, 7)
    shape_all = (VOLUMES, C, NZ, HY, WX)
    channel_scale = jnp.exp(jax.random.uniform(keys[0], (C,), jnp.float32) * math.log(10.0))
    order = jax.random.permutation(keys[1], VOLUMES).astype(jnp.float32)
    volume_scale = jnp.exp(order / max(VOLUMES - 1, 1) * math.log(3.0))
    depth_scale = jnp.exp(jax.random.uniform(keys[2], (VOLUMES, NZ), jnp.float32) * math.log(2.0))
    shared_mix = jax.random.uniform(keys[3], (C,), jnp.float32, -1.0, 1.0)
    own_mix = jax.random.uniform(keys[4], (VOLUMES, C), jnp.float32, -1.0, 1.0)
    scales = volume_scale[:, None, None, None, None] * channel_scale[None, :, None, None, None] * depth_scale[:, None, :, None, None]
    mixing = 0.6 * shared_mix[None, :] + 0.4 * own_mix
    base_values = jax.random.truncated_normal(keys[5], -3.0, 3.0, shape_all, jnp.float32)
    common = jax.random.truncated_normal(keys[6], -3.0, 3.0, (VOLUMES, 1, NZ, HY, WX), jnp.float32)
    core = base_values + mixing[:, :, None, None, None] * common
    return (core * scales).astype(jnp.bfloat16)


def draw_cotangent(key, part):
    keys = jax.random.split(jax.random.fold_in(key, 17), 3)
    shape_all = (VOLUMES, C, NZ, HY, WX)
    shift = 0.4 * jax.random.uniform(keys[0], (C,), jnp.float32, -1.0, 1.0)[None, :] + 0.15 * jax.random.uniform(keys[1], (VOLUMES, C), jnp.float32, -1.0, 1.0)
    noise = jax.random.truncated_normal(keys[2], -3.5, 3.5, shape_all, jnp.float32)
    return (noise + shift[:, :, None, None, None]).astype(jnp.bfloat16)


def scatter_about(stream_key, dims, deviation, reach, kind=jnp.bfloat16):
    entries = jax.random.normal(stream_key, dims, jnp.float32) * deviation
    return jnp.minimum(jnp.maximum(entries, -reach), reach).astype(kind)


def setup_inputs(seed: int = 0) -> dict:
    arg_keys = jax.random.split(jax.random.key(seed), 5)
    return {
        "volumes": draw_volumes(jax.random.fold_in(arg_keys[4], 71), 0),
        "depth_kernel": scatter_about(arg_keys[1], (C, 27), 27 ** -0.5, 1.25, jnp.float32),
        "point_weight": scatter_about(arg_keys[2], (C, C), C ** -0.5, 1.0),
        "cotangent": draw_cotangent(jax.random.fold_in(arg_keys[4], 71), 0),
    }


epsilon = 1e-05
highest = lax.Precision.HIGHEST

def matmul_high(matrix, operand):
    return jnp.matmul(matrix, operand, precision=highest)

def contract_rows(matrix, operand):
    return jnp.einsum('cv,dv->cd', matrix, operand, precision=highest, preferred_element_type=jnp.float32)

def contract_cols(matrix, operand):
    return jnp.einsum('kc,kv->cv', matrix, operand, precision=highest, preferred_element_type=jnp.float32)

def block_diagonal(blocks):
    identity = jnp.eye(blocks.shape[0], dtype=blocks.dtype)
    full_size = blocks.shape[0] * blocks.shape[1]
    return jnp.einsum('gh,gij->gihj', identity, blocks, precision=highest).reshape(full_size, full_size)

def whiten_stats(first_sums, second_sums, voxel_count):
    groups = second_sums.shape[0]
    group_size = second_sums.shape[1]
    average = (first_sums / voxel_count).reshape(groups, group_size)
    identity = jnp.eye(group_size, dtype=second_sums.dtype)
    covariance = second_sums / voxel_count - average[:, :, None] * average[:, None, :] + epsilon * identity
    traces = jnp.trace(covariance, axis1=1, axis2=2)
    normed = covariance / traces[:, None, None]
    project = jnp.broadcast_to(identity, covariance.shape)
    for newton_step in range(NEWTON):
        cubed = matmul_high(matmul_high(project, project), project)
        project = 0.5 * (3.0 * project - matmul_high(cubed, normed))
    whiten_mat = project / jnp.sqrt(traces)[:, None, None]
    offset = jnp.einsum('gij,gj->gi', whiten_mat, average, precision=highest)
    return (whiten_mat, offset)

def adjoint_terms(pull_back, whiten_mat, grad_first, grad_second):
    d_first, d_second = pull_back((grad_second, -grad_first.reshape(whiten_mat.shape[0], whiten_mat.shape[1])))
    adjoint = block_diagonal(jnp.swapaxes(whiten_mat, 1, 2))
    symmetric = block_diagonal(d_second + jnp.swapaxes(d_second, 1, 2))
    return (d_first, adjoint, symmetric)

def gradient_signal(adjoint, d_first, symmetric, grad_part, mixed_part):
    first_term = jnp.dot(adjoint, grad_part, precision=highest, preferred_element_type=jnp.float32)
    third_term = jnp.dot(symmetric, mixed_part, precision=highest, preferred_element_type=jnp.float32)
    return first_term + d_first[:, None] + third_term

def pad_sides(extended):
    return jnp.pad(extended, ((0, 0), (0, 0), (1, 1), (1, 1)))

def tap_cells(padded, tap_index, depth_cells):
    plane_off = tap_index // 9
    row_off = tap_index // 3 % 3
    col_off = tap_index % 3
    height = padded.shape[2] - 2
    width_cells = padded.shape[3] - 2
    return padded[:, plane_off:plane_off + depth_cells, row_off:row_off + height, col_off:col_off + width_cells]

def depth_conv(extended, kernel, depth_cells):
    padded = pad_sides(extended)
    summed = jnp.zeros((extended.shape[0], depth_cells, extended.shape[2], extended.shape[3]), jnp.float32)
    for tap_index in range(27):
        summed = summed + kernel[:, tap_index][:, None, None, None] * tap_cells(padded, tap_index, depth_cells).astype(jnp.float32)
    return summed

def depth_adjoint(grad_ext, kernel, depth_cells):
    padded = pad_sides(grad_ext)
    height = grad_ext.shape[2]
    width_cells = grad_ext.shape[3]
    summed = jnp.zeros((grad_ext.shape[0], depth_cells, height, width_cells), jnp.float32)
    for tap_index in range(27):
        plane_off = 2 - tap_index // 9
        row_off = 2 - tap_index // 3 % 3
        col_off = 2 - tap_index % 3
        summed = summed + kernel[:, tap_index][:, None, None, None] * padded[:, plane_off:plane_off + depth_cells, row_off:row_off + height, col_off:col_off + width_cells]
    return summed

def forward_volume(volume, depth_kernel, point_weight):
    extended = jnp.pad(volume, ((0, 0), (1, 1), (0, 0), (0, 0)))
    hidden = depth_conv(extended, depth_kernel, NZ).astype(jnp.bfloat16).reshape(C, -1)
    mixed_out = jnp.dot(point_weight, hidden, preferred_element_type=jnp.float32).astype(jnp.bfloat16)
    return (extended, hidden, mixed_out)

def reference(volumes, depth_kernel, point_weight, cotangent):
    voxel_count = float(COUNT)

    def stat_step(running, volume):
        mixed_out = forward_volume(volume, depth_kernel, point_weight)[2]
        grouped = mixed_out.reshape(GROUPS, GSIZE, -1).astype(jnp.float32)
        first_new = running[0] + lax.optimization_barrier(jnp.sum(grouped, axis=2)).reshape(C)
        second_new = running[1] + jnp.einsum('giv,gjv->gij', grouped, grouped)
        return ((first_new, second_new), None)
    zero_sums = (jnp.zeros((C,), jnp.float32), jnp.zeros((GROUPS, GSIZE, GSIZE), jnp.float32))
    (first_sums, second_sums), ignored = lax.scan(stat_step, zero_sums, volumes)
    (whiten_mat, offset), pull_back = jax.vjp(partial(whiten_stats, voxel_count=voxel_count), first_sums, second_sums)
    full_white = block_diagonal(whiten_mat)

    def white_step(running, volume_pair):
        volume, grad_in = volume_pair
        mixed_out = forward_volume(volume, depth_kernel, point_weight)[2]
        whitened = (jnp.dot(full_white, mixed_out, precision=highest, preferred_element_type=jnp.float32) - offset.reshape(C)[:, None]).astype(jnp.bfloat16)
        grad_flat = grad_in.reshape(C, -1).astype(jnp.float32)
        grouped = mixed_out.reshape(GROUPS, GSIZE, -1).astype(jnp.float32)
        first_new = running[0] + lax.optimization_barrier(jnp.sum(grad_flat, axis=1))
        second_new = running[1] + jnp.einsum('giv,gjv->gij', grad_flat.reshape(GROUPS, GSIZE, -1), grouped)
        return ((first_new, second_new), whitened.reshape(C, NZ, HY, WX))
    (grad_first, grad_second), whitened_all = lax.scan(white_step, zero_sums, (volumes, cotangent))
    d_first, adjoint, symmetric = adjoint_terms(pull_back, whiten_mat, grad_first, grad_second)
    weight_f = point_weight.astype(jnp.float32)

    def grad_step(running, volume_pair):
        volume, grad_in = volume_pair
        extended, hidden, mixed_out = forward_volume(volume, depth_kernel, point_weight)
        d_mixed = gradient_signal(adjoint, d_first, symmetric, grad_in.reshape(C, -1), mixed_out)
        d_hidden = contract_cols(weight_f, d_mixed).reshape(C, NZ, HY, WX)
        padded_x = pad_sides(extended)
        kernel_terms = jnp.stack([lax.optimization_barrier(jnp.sum(d_hidden * tap_cells(padded_x, tap_index, NZ).astype(jnp.float32), axis=(1, 2, 3))) for tap_index in range(27)], axis=1)
        grad_ext = jnp.pad(d_hidden, ((0, 0), (1, 1), (0, 0), (0, 0)))
        d_volume = depth_adjoint(grad_ext, depth_kernel, NZ).astype(jnp.bfloat16)
        return ((running[0] + contract_rows(d_mixed, hidden), running[1] + kernel_terms), d_volume)
    zero_grads = (jnp.zeros((C, C), jnp.float32), jnp.zeros((C, 27), jnp.float32))
    (d_point, d_kernel), d_volumes = lax.scan(grad_step, zero_grads, (volumes, cotangent))
    scale_out = 1.0 / math.sqrt(voxel_count)
    return (whitened_all, d_volumes, d_point * scale_out, d_kernel * scale_out)
```

```python
import functools
import math

import jax
import jax.numpy as jnp
from jax import lax
from jax.experimental import pallas as pl
from jax.experimental.pallas import tpu as pltpu
from jax.sharding import PartitionSpec as P

GSIZE = 16
NEWTON = 5
EPS = 1e-05
F32 = jnp.float32
BF16 = jnp.bfloat16
HIGHEST = lax.Precision.HIGHEST
NT = (((1,), (1,)), ((), ()))


def mm(left, right):
    return jnp.dot(left, right, precision=HIGHEST, preferred_element_type=F32)


def mm_nt(left, right):
    return lax.dot_general(left, right, NT, precision=HIGHEST, preferred_element_type=F32)


def iota(shape, dim):
    return lax.broadcasted_iota(jnp.int32, shape, dim)


def group_sum(values, low):
    zero = jnp.zeros_like(values)
    first = jnp.sum(jnp.where(low, values, zero), keepdims=True)
    second = jnp.sum(jnp.where(low, zero, values), keepdims=True)
    return jnp.where(low, first, second)


def stats_and_adjoint(packed, voxel_count):
    channels = 2 * GSIZE
    lane = iota((GSIZE, 128), 1)
    in_zero = (lane < 96) & (((lane < 64) & (lane % 32 < 16)) | ((lane >= 64) & (lane % 16 < 8)))
    in_one = (lane < 96) & jnp.logical_not(in_zero)
    tile = packed[0:GSIZE]
    none = jnp.zeros_like(tile)
    full = jnp.concatenate([jnp.where(in_zero, tile, none), jnp.where(in_one, tile, none)], axis=0)
    second = full[:, 0:32]
    cross = full[:, 32:64]
    low_col = iota((channels, 1), 0) < GSIZE
    avg_col = jnp.where(low_col, full[:, 64:65], full[:, 72:73]) / voxel_count
    gf_col = jnp.where(low_col, full[:, 80:81], full[:, 88:89])
    avg_row = packed[GSIZE : GSIZE + 1, 0:32] / voxel_count
    gf_row = packed[GSIZE : GSIZE + 1, 32:64]
    rows = iota((channels, channels), 0)
    cols = iota((channels, channels), 1)
    low = rows < GSIZE
    same = low == (cols < GSIZE)
    eye = jnp.where(rows == cols, 1.0, 0.0).astype(F32)
    zero = jnp.zeros((channels, channels), F32)
    cov = second / voxel_count - jnp.where(same, avg_col * avg_row, zero) + EPS * eye
    traces = group_sum(cov * eye, low)
    normed = cov / traces
    root = 1.0 / jnp.sqrt(traces)
    project = 1.5 * eye - 0.5 * normed
    kept = []
    for _ in range(NEWTON - 1):
        square = mm(project, project)
        by_n = mm(project, normed)
        cube_n = mm(square, by_n)
        kept.append((project, square, by_n, mm(square, normed), mm(square, project)))
        project = 1.5 * project - 0.5 * cube_n
    whiten = project * root
    offset = jnp.sum(whiten * avg_row, axis=1, keepdims=True)

    grad = cross - jnp.where(same, avg_col * gf_row, zero)
    d_traces = group_sum(grad * project, low) * (-0.5) * root / traces
    grad = grad * root
    d_normed = zero
    for before, square, by_n, square_n, cube in reversed(kept):
        d_normed = d_normed - 0.5 * mm(cube, grad)
        grad = 1.5 * grad - 0.5 * (
            mm(grad, square_n) + mm(before, mm(grad, by_n)) + mm(square, mm(grad, normed))
        )
    d_normed = d_normed - 0.5 * grad
    d_traces = d_traces - group_sum(d_normed * normed, low) / traces
    d_cov = d_normed / traces + d_traces * eye
    sym = d_cov + mm_nt(eye, d_cov)
    d_avg = -jnp.sum(sym * avg_row, axis=1, keepdims=True) - jnp.sum(
        whiten * gf_row, axis=1, keepdims=True
    )
    del gf_col
    return whiten, offset, sym / voxel_count, d_avg / voxel_count


def split(values):
    high = values.astype(BF16)
    return high, (values - high.astype(F32)).astype(BF16)


def kernel(
    samples, spaces, voxel_count,
    vol_ref, taps_ref, weight_ref, cot_ref,
    white_ref, dvol_ref, dpoint_ref, dkernel_ref,
    xf, dhf, zs, nf, hf, kt, vhalo, hnat, dstage, dhalo, rmat,
    sum1a, sum1b, sum2a, sum2b,
    hv_send, hv_recv, hd_send, hd_recv,
    s1a, r1a, s1b, r1b, s2a, r2a, s2b, r2b,
):
    channels, depth, height, width = vol_ref.shape[1:]
    rows_all = depth * height
    padded = height + 2
    me = lax.axis_index("sample")
    pos = lax.axis_index("space")
    first_dev = pos == 0
    last_dev = pos == spaces - 1

    barrier = pltpu.get_barrier_semaphore()
    for step in range(1, samples):
        pl.semaphore_signal(
            barrier, inc=1, device_id=(lax.rem(me + step, samples), pos),
            device_id_type=pl.DeviceIdType.MESH,
        )
    for step in range(1, spaces):
        pl.semaphore_signal(
            barrier, inc=1, device_id=(me, lax.rem(pos + step, spaces)),
            device_id_type=pl.DeviceIdType.MESH,
        )

    def remote(src, dst, send, recv, target):
        return pltpu.make_async_remote_copy(
            src_ref=src, dst_ref=dst, send_sem=send, recv_sem=recv,
            device_id=target, device_id_type=pl.DeviceIdType.MESH,
        )

    def exchange_sample(buf, send, recv):
        return [
            remote(buf.at[me], buf.at[me], send.at[k], recv.at[k], (lax.rem(me + k, samples), pos))
            for k in range(1, samples)
        ]

    def exchange_space(buf, send, recv):
        return [
            remote(buf.at[pos], buf.at[pos], send.at[k], recv.at[k], (me, lax.rem(pos + k, spaces)))
            for k in range(1, spaces)
        ]

    def total(buf, count):
        result = buf[0]
        for k in range(1, count):
            result = result + buf[k]
        return result

    lane32 = iota((channels, width), 1)

    def put_shifted(dst, row, value):
        zero = jnp.zeros_like(value)
        dst[1, row] = value
        dst[0, row] = jnp.where(lane32 == 0, zero, pltpu.roll(value, 1, 1))
        dst[2, row] = jnp.where(lane32 == width - 1, zero, pltpu.roll(value, width - 1, 1))

    def zero_plane(dst, plane):
        def body(h, carry):
            for e in range(3):
                dst[e, plane * padded + 1 + h] = jnp.zeros((channels, width), F32)
            return carry
        lax.fori_loop(0, height, body, 0)

    def to_natural(src):
        def body(c, carry):
            nf[pl.ds(c * rows_all, rows_all), :] = (
                src[0, c].reshape(rows_all, width).astype(F32)
            )
            return carry
        lax.fori_loop(0, channels, body, 0)

    to_natural(vol_ref)

    def own_rows(i, carry):
        for j in range(4):
            zh = i * 4 + j
            row = (zh // height + 1) * padded + 1 + lax.rem(zh, height)
            put_shifted(xf, row, nf[pl.ds(zh, channels, stride=rows_all), :])
        return carry
    lax.fori_loop(0, rows_all // 4, own_rows, 0)

    pl.semaphore_wait(barrier, samples - 1 + spaces - 1)

    up = (me, pos + 1)
    down = (me, pos - 1)
    v_up = remote(vol_ref.at[0, :, depth - 1], vhalo.at[0], hv_send.at[0], hv_recv.at[0], up)
    v_down = remote(vol_ref.at[0, :, 0], vhalo.at[1], hv_send.at[1], hv_recv.at[1], down)

    @pl.when(jnp.logical_not(last_dev))
    def _():
        v_up.start()

    @pl.when(jnp.logical_not(first_dev))
    def _():
        v_down.start()

    for buf in (xf, dhf):
        def edge(plane, carry, buf=buf):
            for e in range(3):
                buf[e, plane * padded] = jnp.zeros((channels, width), F32)
                buf[e, plane * padded + padded - 1] = jnp.zeros((channels, width), F32)
            return carry
        lax.fori_loop(0, depth + 2, edge, 0)

    for t in range(27):
        kt[t] = jnp.broadcast_to(taps_ref[:, t : t + 1], (channels, width))

    def conv_rows(src, z, g, hb, flip):
        sub = pl.ds(pl.multiple_of(g * 8, 8), 8)
        taps = [kt[t, sub, :] for t in range(27)]
        accs = [None] * 8
        for r in range(10):
            for a in range(3):
                for e in range(3):
                    value = src[e, (z + a) * padded + hb * 8 + r, sub, :]
                    for b in range(3):
                        h = r - b
                        if 0 <= h < 8:
                            t = 9 * a + 3 * b + e
                            term = taps[26 - t if flip else t] * value
                            accs[h] = term if accs[h] is None else accs[h] + term
        return sub, accs

    def forward(z):
        def body(i, carry):
            g, hb = i // 2, lax.rem(i, 2)
            sub, accs = conv_rows(xf, z, g, hb, False)
            for h in range(8):
                hf[z * height + hb * 8 + h, sub, :] = accs[h]
            return carry
        lax.fori_loop(0, channels // 8 * 2, body, 0)

    def plane_loop(first, count, fn):
        def body(z, carry):
            fn(z)
            return carry
        lax.fori_loop(first, first + count, body, 0)

    plane_loop(1, depth - 2, forward)

    to_natural(cot_ref)

    def cot_rows(i, carry):
        for j in range(4):
            zh = i * 4 + j
            lanes = pl.ds(pl.multiple_of(zh * width, width), width)
            zs[32:64, lanes] = nf[pl.ds(zh, channels, stride=rows_all), :].astype(BF16)
            zs[64:80, lanes] = jnp.ones((16, width), BF16)
            zs[80:96, lanes] = jnp.zeros((16, width), BF16)
        return carry
    lax.fori_loop(0, rows_all // 4, cot_rows, 0)

    def take_halo(which, plane):
        def cast(c, carry):
            hnat[pl.ds(c * height, height), :] = vhalo[which, c].astype(F32)
            return carry
        lax.fori_loop(0, channels, cast, 0)

        def body(h, carry):
            put_shifted(xf, plane * padded + 1 + h, hnat[pl.ds(h, channels, stride=height), :])
            return carry
        lax.fori_loop(0, height, body, 0)

    @pl.when(jnp.logical_not(first_dev))
    def _():
        v_up.wait_recv()
        take_halo(0, 0)

    @pl.when(first_dev)
    def _():
        zero_plane(xf, 0)

    @pl.when(jnp.logical_not(last_dev))
    def _():
        v_down.wait_recv()
        take_halo(1, depth + 1)

    @pl.when(last_dev)
    def _():
        zero_plane(xf, depth + 1)

    forward(0)
    forward(depth - 1)

    chunk_rows = 8
    chunk = chunk_rows * width
    weight = weight_ref[...]

    def mix(i, gram):
        lanes = pl.ds(pl.multiple_of(i * chunk, chunk), chunk)
        hidden = jnp.concatenate(
            [hf[i * chunk_rows + r] for r in range(chunk_rows)], axis=1
        ).astype(BF16)
        zs[96:128, lanes] = hidden
        mixed = jnp.dot(weight, hidden, preferred_element_type=F32).astype(BF16)
        zs[0:32, lanes] = mixed
        block = zs[:, lanes]
        return gram + lax.dot_general(block, block, NT, preferred_element_type=F32)
    gram = lax.fori_loop(0, rows_all // chunk_rows, mix, jnp.zeros((128, 128), F32))

    lane16 = iota((GSIZE, 128), 1)
    stats_low = (lane16 < 96) & (
        ((lane16 < 64) & (lane16 % 32 < 16)) | ((lane16 >= 64) & (lane16 % 16 < 8))
    )
    sum1a[me, 0:GSIZE, :] = jnp.where(
        stats_low, gram[0:GSIZE], gram[GSIZE : 2 * GSIZE]
    )
    sum1a[me, GSIZE : GSIZE + 8, :] = gram[64:72]
    copies1a = exchange_sample(sum1a, s1a, r1a)
    for copy in copies1a:
        copy.start()
    for copy in copies1a:
        copy.wait_recv()
    sum1b[pos] = total(sum1a, samples)
    copies1b = exchange_space(sum1b, s1b, r1b)
    for copy in copies1b:
        copy.start()
    for copy in copies1b:
        copy.wait_recv()
    packed = total(sum1b, spaces)

    whiten, offset, sym, d_first = stats_and_adjoint(packed, voxel_count)
    none32 = jnp.zeros((channels, channels), F32)
    lane_one = iota((channels, 64), 1) == 0
    tail = jnp.zeros((channels, 64), F32)
    signal = jnp.concatenate([sym, whiten, jnp.where(lane_one, d_first, tail)], axis=1)
    rmat[...] = signal
    to_hidden = lax.dot_general(
        weight.astype(F32), signal, (((0,), (0,)), ((), ())),
        precision=HIGHEST, preferred_element_type=F32,
    )
    to_white = jnp.concatenate([whiten, none32, jnp.where(lane_one, -offset, tail)], axis=1)
    high, rest = split(jnp.concatenate([to_white, to_hidden], axis=0))
    apply_mat = jnp.concatenate([high, rest], axis=0)

    def apply_plane(z, stage):
        for half in range(height // chunk_rows):
            start = z * height + half * chunk_rows
            lanes = pl.ds(pl.multiple_of(start * width, chunk), chunk)
            both = jnp.dot(apply_mat, zs[:, lanes], preferred_element_type=F32)
            both = both[0:64] + both[64:128]
            for r in range(chunk_rows):
                part = both[:, r * width : (r + 1) * width]
                nf[pl.ds(start + r, channels, stride=rows_all), :] = part[0:32]
                h = half * chunk_rows + r
                put_shifted(dhf, (z + 1) * padded + 1 + h, part[32:64])
                if stage is not None:
                    dstage[stage, h] = part[32:64].astype(BF16)

    apply_plane(0, 0)
    apply_plane(depth - 1, 1)
    d_up = remote(dstage.at[1], dhalo.at[0], hd_send.at[0], hd_recv.at[0], up)
    d_down = remote(dstage.at[0], dhalo.at[1], hd_send.at[1], hd_recv.at[1], down)

    @pl.when(jnp.logical_not(last_dev))
    def _():
        d_up.start()

    @pl.when(jnp.logical_not(first_dev))
    def _():
        d_down.start()

    plane_loop(1, depth - 2, lambda z: apply_plane(z, None))

    lane8 = iota((8, 128), 1)

    def tap_grads(g, carry):
        sub = pl.ds(pl.multiple_of(g * 8, 8), 8)

        def body(i, accs):
            z, hb = i // 2, lax.rem(i, 2)
            accs = list(accs)
            grads = [dhf[1, (z + 1) * padded + 1 + hb * 8 + h, sub, :] for h in range(8)]
            for r in range(10):
                for a in range(3):
                    for e in range(3):
                        value = xf[e, (z + a) * padded + hb * 8 + r, sub, :]
                        for b in range(3):
                            h = r - b
                            if 0 <= h < 8:
                                t = 9 * a + 3 * b + e
                                accs[t] = accs[t] + grads[h] * value
            return tuple(accs)

        accs = lax.fori_loop(0, depth * 2, body, (jnp.zeros((8, width), F32),) * 27)
        merged = jnp.zeros((8, 128), F32)
        for t in range(27):
            merged = jnp.where(
                lane8 == 96 + t, jnp.sum(accs[t], axis=1, keepdims=True), merged
            )
        sum2a[me, sub, :] = merged
        return carry
    lax.fori_loop(0, channels // 8, tap_grads, 0)

    lane_p = iota((channels, 128), 1)
    sum2a[me] = jnp.where(lane_p < 96, gram[96:128], sum2a[me])
    copies2a = exchange_sample(sum2a, s2a, r2a)
    for copy in copies2a:
        copy.start()

    def from_natural(dst):
        def body(c, carry):
            dst[0, c] = nf[pl.ds(c * rows_all, rows_all), :].astype(BF16).reshape(
                depth, height, width
            )
            return carry
        lax.fori_loop(0, channels, body, 0)

    from_natural(white_ref)

    def backward(z):
        def body(i, carry):
            g, hb = i // 2, lax.rem(i, 2)
            sub, accs = conv_rows(dhf, z, g, hb, True)
            for h in range(8):
                hf[z * height + hb * 8 + h, sub, :] = accs[h]
            return carry
        lax.fori_loop(0, channels // 8 * 2, body, 0)

    plane_loop(1, depth - 2, backward)

    for copy in copies2a:
        copy.wait_recv()
    sum2b[pos] = total(sum2a, samples)
    copies2b = exchange_space(sum2b, s2b, r2b)
    for copy in copies2b:
        copy.start()

    def take_dhalo(which, plane):
        def body(h, carry):
            put_shifted(dhf, plane * padded + 1 + h, dhalo[which, h].astype(F32))
            return carry
        lax.fori_loop(0, height, body, 0)

    @pl.when(jnp.logical_not(first_dev))
    def _():
        d_up.wait_recv()
        take_dhalo(0, 0)

    @pl.when(first_dev)
    def _():
        zero_plane(dhf, 0)

    @pl.when(jnp.logical_not(last_dev))
    def _():
        d_down.wait_recv()
        take_dhalo(1, depth + 1)

    @pl.when(last_dev)
    def _():
        zero_plane(dhf, depth + 1)

    backward(0)
    backward(depth - 1)

    def out_rows(i, carry):
        for j in range(4):
            zh = i * 4 + j
            nf[pl.ds(zh, channels, stride=rows_all), :] = hf[zh]
        return carry
    lax.fori_loop(0, rows_all // 4, out_rows, 0)
    from_natural(dvol_ref)

    for copy in copies2b:
        copy.wait_recv()
    sums = total(sum2b, spaces)
    scale_out = 1.0 / math.sqrt(voxel_count)
    grams = jnp.where(lane_p < 65, sums, jnp.zeros_like(sums))
    dpoint_ref[...] = mm_nt(rmat[...], grams) * scale_out
    dkernel_ref[...] = sums[:, 96:123] * scale_out

    for copy in copies1a + copies1b + copies2a + copies2b:
        copy.wait_send()

    @pl.when(jnp.logical_not(last_dev))
    def _():
        v_up.wait_send()
        d_up.wait_send()

    @pl.when(jnp.logical_not(first_dev))
    def _():
        v_down.wait_send()
        d_down.wait_send()


def on_device(samples, spaces, volumes, depth_kernel, point_weight, cotangent):
    _, channels, depth, height, width = volumes.shape
    voxels = depth * height * width
    voxel_count = float(voxels * samples * spaces)
    rows = (depth + 2) * (height + 2)
    dma = pltpu.SemaphoreType.DMA
    vmem = pl.BlockSpec(memory_space=pltpu.VMEM)
    big = jax.ShapeDtypeStruct(volumes.shape, BF16)
    return pl.pallas_call(
        functools.partial(kernel, samples, spaces, voxel_count),
        out_shape=(
            big,
            big,
            jax.ShapeDtypeStruct(point_weight.shape, F32),
            jax.ShapeDtypeStruct(depth_kernel.shape, F32),
        ),
        in_specs=[vmem] * 4,
        out_specs=(vmem,) * 4,
        scratch_shapes=[
            pltpu.VMEM((3, rows, channels, width), F32),
            pltpu.VMEM((3, rows, channels, width), F32),
            pltpu.VMEM((128, voxels), BF16),
            pltpu.VMEM((channels * depth * height, width), F32),
            pltpu.VMEM((depth * height, channels, width), F32),
            pltpu.VMEM((27, channels, width), F32),
            pltpu.VMEM((2, channels, height, width), BF16),
            pltpu.VMEM((channels * height, width), F32),
            pltpu.VMEM((2, height, channels, width), BF16),
            pltpu.VMEM((2, height, channels, width), BF16),
            pltpu.VMEM((channels, 128), F32),
            pltpu.VMEM((samples, 24, 128), F32),
            pltpu.VMEM((spaces, 24, 128), F32),
            pltpu.VMEM((samples, channels, 128), F32),
            pltpu.VMEM((spaces, channels, 128), F32),
            dma((2,)), dma((2,)), dma((2,)), dma((2,)),
            dma((samples,)), dma((samples,)), dma((spaces,)), dma((spaces,)),
            dma((samples,)), dma((samples,)), dma((spaces,)), dma((spaces,)),
        ],
        compiler_params=pltpu.CompilerParams(
            collective_id=0, has_side_effects=True, vmem_limit_bytes=44 * 1024 * 1024
        ),
    )(volumes, depth_kernel, point_weight, cotangent)


def solution(mesh):
    big = P("sample", None, "space", None, None)
    body = functools.partial(on_device, mesh.shape["sample"], mesh.shape["space"])
    return jax.shard_map(
        body, mesh=mesh, in_specs=(big, P(), P(), big), out_specs=(big, big, P(), P()),
        check_vma=False,
    )
```
